512 devices in a mesh: band: 16 (over y, x_hi, core), pencil: 32 (over x_lo, z).
Axes of the slice: x: 4 (x_hi: 2, x_lo: 2; x = x_hi * 2 + x_lo), y: 4, z: 16, core: 2. Of those that a mesh axis runs over, the one named last changes fastest.
Arguments:
- panels: bfloat16 [1024, 96, 8, 128], P('band', 'pencil'), may hold values from -7 to 7
- potential: float32 [96, 8, 128], P('pencil'), may hold values from -1 to 1
- plan: int32 [16], replicated, may hold values from 0 to 15, each once
Outputs:
- projected: bfloat16 [1024, 96, 8, 128], P('band', 'pencil')
The draws below stay inside these ranges and needn't reach their ends.
Inputs may be any that keep to these rules, and one draw needn't show every extreme that they name: `plan`: each band group's turn appears once.
All inputs are finite; a program needn't handle non-finite values.
Results may differ from the reference program's by a relative error of at most 0.009.
Values may be sent and summed in bfloat16 or wider, within the bound.
No kernel may reach another device: no remote copies, remote signals or barrier semaphores. Data moves between devices by JAX's collectives and lax.ppermute only.
A program may use at most 64 MiB of HBM per device.

```python
import jax
import jax.numpy as jnp
from jax import lax

ORB = 64
CY = 8
CZ = 128
NBANDS = 16
NORB = 1024
NX = 96
NCELL = 98304


def draw_panels(key, part):
    key = jax.random.fold_in(key, 7)
    first_key, second_key = jax.random.split(key)
    own = jax.random.normal(first_key, (NORB, NX, CY, CZ), jnp.float32)
    common = jax.random.normal(second_key, (ORB, NX, CY, CZ), jnp.float32)
    mixing = 0.7
    values = own + mixing * jnp.tile(common, (NBANDS, 1, 1, 1))
    return jnp.clip(values, -7.0, 7.0).astype(jnp.bfloat16)


def block_levels(stream_key, shape, shards, low, largest):
    def one(position, parts):
        draws = jax.random.uniform(jax.random.fold_in(jax.random.fold_in(stream_key, 6), position), (parts,), jnp.float32, low / len(shards), largest / len(shards))
        return jnp.repeat(jnp.exp(draws), shape[position] // parts).reshape((-1,) + (1,) * (len(shape) - position - 1))

    factor_of = one(*shards[0])
    for cut in shards[1:]:
        factor_of = factor_of * one(*cut)
    return factor_of


def setup_inputs(seed: int = 0) -> dict:
    key_of = jax.random.split(jax.random.key(seed), 4)
    panels = draw_panels(jax.random.fold_in(key_of[3], 71), 0)
    potential = jnp.clip(jax.random.uniform(key_of[1], (NX, CY, CZ), jnp.float32, -1.0, 1.0) * block_levels(key_of[1], (NX, CY, CZ), ((0, 32),), -0.4, 0.0), -1.0, 1.0)
    plan = jax.random.permutation(key_of[2], NBANDS).astype(jnp.int32)
    return {"panels": panels, "potential": potential, "plan": plan}


WEIGHTS = (-49.0 / 18.0, 1.5, -0.15, 1.0 / 90.0)
CENTRE = 6.05
HALFWIDTH = 4.05


def laplace(field):
    total = 3.0 * WEIGHTS[0] * field
    for dist in range(1, 4):
        for axis in (1, 2, 3):
            total = total + WEIGHTS[dist] * (jnp.roll(field, dist, axis) + jnp.roll(field, -dist, axis))
    return total


def hamiltonian(field, potential):
    return -0.5 * laplace(field) + potential[None] * field


def filter_group(group, potential):
    start = group.astype(jnp.float32)
    first = ((hamiltonian(start, potential) - CENTRE * start) / HALFWIDTH).astype(jnp.bfloat16)
    firstf = first.astype(jnp.float32)
    second = 2.0 * (hamiltonian(firstf, potential) - CENTRE * firstf) / HALFWIDTH - start
    return second.astype(jnp.bfloat16)


def reference(panels, potential, plan):
    grouped = panels.reshape(NBANDS, ORB, NX, CY, CZ)
    filtered = lax.map(lambda group: filter_group(group, potential), grouped)
    matrix = panels.reshape(NORB, NCELL)
    fmat = filtered.reshape(NBANDS, ORB, NCELL)

    def project(index):
        mine = fmat[index]
        overl = jnp.dot(matrix, mine.T, preferred_element_type=jnp.float32)
        before = jnp.repeat(plan < plan[index], ORB)
        coef = jnp.where(before[:, None], overl * (1.0 / NCELL), 0.0).astype(jnp.bfloat16)
        proj = jnp.dot(coef.T, matrix, preferred_element_type=jnp.float32)
        return (mine.astype(jnp.float32) - proj).astype(jnp.bfloat16)

    result = lax.map(project, jnp.arange(NBANDS, dtype=jnp.int32))
    return result.reshape(NORB, NX, CY, CZ)
```

```python
import jax
import jax.numpy as jnp
from jax import lax
from jax.sharding import Mesh, PartitionSpec as P

WEIGHTS = (-49.0 / 18.0, 1.5, -0.15, 1.0 / 90.0)
CENTRE = 6.05
HALFWIDTH = 4.05
SIZES = (("y", 4), ("xh", 2), ("core", 2), ("xl", 2), ("z1", 4), ("z0", 4))
BAND = ("y", "xh", "core")
PENCIL = ("xl", "z1", "z0")
NEAR = ("xl", "z0")
BF16 = jnp.bfloat16
F32 = jnp.float32


def halos(shard):
    size = lax.axis_size(PENCIL)
    up = [(i, (i + 1) % size) for i in range(size)]
    down = [(j, i) for i, j in up]
    return lax.ppermute(shard, PENCIL, up), lax.ppermute(shard, PENCIL, down)


def hamiltonian(field_low, before, after, potential):
    extended = jnp.concatenate([before, field_low, after], axis=1)
    field = field_low.astype(F32)
    planes = field.shape[1]
    total = 3.0 * WEIGHTS[0] * field
    for dist in range(1, 4):
        upper = extended[:, 3 + dist : 3 + dist + planes].astype(F32)
        lower = extended[:, 3 - dist : 3 - dist + planes].astype(F32)
        total = total + WEIGHTS[dist] * (upper + lower)
        for axis in (2, 3):
            ahead = jnp.roll(field_low, dist, axis).astype(F32)
            behind = jnp.roll(field_low, -dist, axis).astype(F32)
            total = total + WEIGHTS[dist] * (ahead + behind)
    return (field, -0.5 * total + potential[None] * field)


def gather_bands(rows):
    y, xh, core = (lax.axis_index(a) for a in BAND)
    ny = lax.axis_size("y")
    same = lax.all_gather(rows, "y", axis=0, tiled=True)
    others = []
    for dy in range(ny):
        pairs = [(a * 2 + b, ((a + dy) % ny) * 2 + 1 - b) for a in range(ny) for b in range(2)]
        others.append(lax.ppermute(rows, ("y", "xh"), pairs))
    mine = jnp.concatenate([same] + others, axis=0)
    theirs = lax.ppermute(mine, "core", [(0, 1), (1, 0)])
    step = jnp.arange(ny)
    ids = jnp.concatenate([(step * 2 + xh) * 2, (((y - step) % ny) * 2 + 1 - xh) * 2])
    return mine, theirs, jnp.concatenate([ids + core, ids + 1 - core])


def body(panels, potential, plan):
    orbitals = panels.shape[0]
    local_rows = panels.reshape(orbitals, -1)
    scale = 1.0 / (local_rows.shape[1] * lax.axis_size(PENCIL))
    before, after = halos(panels)
    mine, theirs, ids = gather_bands(local_rows)
    start, applied = hamiltonian(panels, before, after, potential)
    first = ((applied - CENTRE * start) / HALFWIDTH).astype(BF16)
    before, after = halos(first)
    firstf, applied_two = hamiltonian(first, before, after, potential)
    filtered = (2.0 * (applied_two - CENTRE * firstf) / HALFWIDTH - start).astype(BF16)
    local_filtered = filtered.reshape(orbitals, -1)
    gathered = jnp.concatenate([mine, theirs], axis=0)
    partial = lax.dot_general(
        local_filtered, gathered, (((1,), (1,)), ((), ())), preferred_element_type=F32
    )
    band = sum(lax.axis_index(a) * s for a, s in zip(BAND, (4, 2, 1)))
    earlier = jnp.repeat(plan[ids] < plan[band], orbitals, total_repeat_length=gathered.shape[0])
    near = lax.axis_size(NEAR)
    pieces = partial.astype(BF16).reshape(near, orbitals // near, -1)
    pieces = lax.all_to_all(pieces, NEAR, 0, 0)
    share = jnp.sum(pieces.astype(F32), axis=0).astype(BF16)
    far = lax.axis_size("z1")
    shares = lax.all_to_all(jnp.broadcast_to(share[None], (far,) + share.shape), "z1", 0, 0)
    summed = jnp.sum(shares.astype(F32), axis=0)
    part = jnp.where(earlier[None, :], summed * scale, 0.0).astype(BF16)
    coef = lax.all_to_all(jnp.broadcast_to(part[None], (near,) + part.shape), NEAR, 0, 0)
    coef = coef.reshape(orbitals, -1)
    removed = lax.dot_general(coef, gathered, (((1,), (0,)), ((), ())), preferred_element_type=F32)
    result = (local_filtered.astype(F32) - removed).astype(BF16)
    return result.reshape(panels.shape)


def solution(mesh):
    fine = Mesh(mesh.devices.reshape([s for _, s in SIZES]), [n for n, _ in SIZES])
    in_specs = (P(BAND, PENCIL, None, None), P(PENCIL, None, None), P())
    out_specs = P(BAND, PENCIL, None, None)
    return jax.shard_map(body, mesh=fine, in_specs=in_specs, out_specs=out_specs, check_vma=False)
```

```python
import functools

import jax
import jax.numpy as jnp
from jax import lax
from jax.experimental import pallas as pl
from jax.experimental.pallas import tpu as pltpu
from jax.sharding import Mesh, PartitionSpec as P

WEIGHTS = (-49.0 / 18.0, 1.5, -0.15, 1.0 / 90.0)
CENTRE = 6.05
HALFWIDTH = 4.05
SIZES = (("y", 4), ("xh", 2), ("core", 2), ("xl", 2), ("z1", 4), ("z0", 4))
BAND = ("y", "xh", "core")
PENCIL = ("xl", "z1", "z0")
NEAR = ("xl", "z0")
BF16 = jnp.bfloat16
F32 = jnp.float32
LANES = 128
ROWS = 8
REACH = 3
VMEM = pl.BlockSpec(memory_space=pltpu.VMEM)
SMEM = pl.BlockSpec(memory_space=pltpu.SMEM)


def halos(shard):
    size = lax.axis_size(PENCIL)
    up = [(i, (i + 1) % size) for i in range(size)]
    down = [(j, i) for i, j in up]
    return lax.ppermute(shard, PENCIL, up), lax.ppermute(shard, PENCIL, down)


def stencil_kernel(second, before, mid, after, pot, *rest):
    if second:
        start, out, ext = rest
    else:
        out, ext = rest
    width = mid.shape[1]
    slices = width // LANES
    ext[:, :width] = before[...].astype(F32)
    ext[:, width : 2 * width] = mid[...].astype(F32)
    ext[:, 2 * width :] = after[...].astype(F32)
    factor = 2.0 if second else 1.0
    centre = (pot[...] - 1.5 * WEIGHTS[0] - CENTRE) * (factor / HALFWIDTH)

    def at(index):
        return ext[:, index * LANES : (index + 1) * LANES]

    for s in range(slices):
        plane, row = divmod(s, ROWS)
        own = at(slices + s)
        total = centre[s : s + 1, :] * own
        for dist in range(1, REACH + 1):
            near = at(slices + s + ROWS * dist) + at(slices + s - ROWS * dist)
            base = slices + plane * ROWS
            near = near + at(base + (row + dist) % ROWS) + at(base + (row - dist) % ROWS)
            near = near + pltpu.roll(own, dist, 1) + pltpu.roll(own, LANES - dist, 1)
            total = total + (-0.5 * factor * WEIGHTS[dist] / HALFWIDTH) * near
        cells = slice(s * LANES, (s + 1) * LANES)
        if second:
            total = total - start[:, cells].astype(F32)
        out[:, cells] = total.astype(BF16)


def stencil(before, mid, after, pot, start=None):
    args = [before, mid, after, pot] + ([] if start is None else [start])
    return pl.pallas_call(
        functools.partial(stencil_kernel, start is not None),
        out_shape=jax.ShapeDtypeStruct(mid.shape, BF16),
        in_specs=[VMEM] * len(args),
        out_specs=VMEM,
        scratch_shapes=[pltpu.VMEM((mid.shape[0], 3 * mid.shape[1]), F32)],
        compiler_params=pltpu.CompilerParams(vmem_limit_bytes=16 * 2**20),
        cost_estimate=pl.CostEstimate(flops=8_000_000, bytes_accessed=2_000_000, transcendentals=0),
        name="stencil_second" if start is not None else "stencil_first",
    )(*args)


def share_kernel(pieces, out):
    total = jnp.sum(pieces[...].astype(F32), axis=0).astype(BF16)
    for k in range(out.shape[0]):
        out[k] = total


def coef_kernel(scale, plan, place, pieces, out):
    total = jnp.sum(pieces[...].astype(F32), axis=0) * scale
    y, xh, core = place[0], place[1], place[2]
    turn = plan[4 * y + 2 * xh + core]
    bands = plan.shape[0]
    orbitals = total.shape[1] // bands
    low = lax.broadcasted_iota(jnp.int32, (total.shape[0], LANES), 1) < orbitals

    def earlier(block):
        group, source = divmod(block, bands // 4)
        side = xh if group < 2 else 1 - xh
        parity = core if group % 2 == 0 else 1 - core
        return (plan[4 * source + 2 * side + parity] < turn).astype(jnp.int32)

    for c in range(total.shape[1] // LANES):
        keep = jnp.where(low, earlier(2 * c), earlier(2 * c + 1)) > 0
        cells = slice(c * LANES, (c + 1) * LANES)
        part = jnp.where(keep, total[:, cells], 0.0).astype(BF16)
        for k in range(out.shape[0]):
            out[k, :, cells] = part


def along_y(block):
    count = lax.axis_size("y")
    wide = jnp.broadcast_to(block[None], (count,) + block.shape)
    return lax.all_to_all(wide, "y", 0, 0).reshape(count * block.shape[0], -1)


def swap_cores(block):
    return lax.ppermute(block, "core", [(0, 1), (1, 0)])


def body(panels, potential, plan):
    orbitals = panels.shape[0]
    rows = panels.reshape(orbitals, -1)
    pot = potential.reshape(-1, LANES)
    scale = 1.0 / (rows.shape[1] * lax.axis_size(PENCIL))
    near, far = lax.axis_size(NEAR), lax.axis_size("z1")
    before, after = halos(rows)
    swapped = lax.ppermute(rows, "xh", [(0, 1), (1, 0)])
    same = along_y(rows)
    swapped, before, after = lax.optimization_barrier((swapped, before, after))
    other = along_y(swapped)
    first = stencil(before, rows, after, pot)
    before, after = halos(first)
    same_core = swap_cores(same)
    other, before, after = lax.optimization_barrier((other, before, after))
    other_core = swap_cores(other)
    filtered = stencil(before, first, after, pot, rows)
    blocks = [same, same_core, other, other_core]

    def margins(other):
        return lax.dot_general(
            filtered, other, (((1,), (1,)), ((), ())), preferred_element_type=F32
        ).astype(BF16)

    partial = jnp.concatenate([margins(block) for block in blocks], axis=1)
    pieces = lax.all_to_all(partial.reshape(near, orbitals // near, -1), NEAR, 0, 0)
    share = (orbitals // near, partial.shape[1])
    shares = pl.pallas_call(
        share_kernel,
        out_shape=jax.ShapeDtypeStruct((far,) + share, BF16),
        in_specs=[VMEM],
        out_specs=VMEM,
        name="share",
    )(pieces)
    shares = lax.all_to_all(shares, "z1", 0, 0)
    place = jnp.stack([lax.axis_index(a) for a in BAND]).astype(jnp.int32)
    coef = pl.pallas_call(
        functools.partial(coef_kernel, scale),
        out_shape=jax.ShapeDtypeStruct((near,) + share, BF16),
        in_specs=[SMEM, SMEM, VMEM],
        out_specs=VMEM,
        name="coef",
    )(plan, place, shares)
    coef = lax.all_to_all(coef, NEAR, 0, 0).reshape(orbitals, -1)
    width = same.shape[0]
    removed = jnp.zeros(rows.shape, F32)
    for k, block in enumerate(blocks):
        removed = removed + lax.dot_general(
            coef[:, k * width : (k + 1) * width], block, (((1,), (0,)), ((), ())),
            preferred_element_type=F32,
        )
    result = (filtered.astype(F32) - removed).astype(BF16)
    return result.reshape(panels.shape)


def solution(mesh):
    fine = Mesh(mesh.devices.reshape([s for _, s in SIZES]), [n for n, _ in SIZES])
    in_specs = (P(BAND, PENCIL, None, None), P(PENCIL, None, None), P())
    out_specs = P(BAND, PENCIL, None, None)
    return jax.shard_map(body, mesh=fine, in_specs=in_specs, out_specs=out_specs, check_vma=False)
```

```python
import functools

import jax
import jax.numpy as jnp
from jax import lax
from jax.experimental import pallas as pl
from jax.experimental.pallas import tpu as pltpu
from jax.sharding import Mesh, PartitionSpec as P

WEIGHTS = (-49.0 / 18.0, 1.5, -0.15, 1.0 / 90.0)
CENTRE = 6.05
HALFWIDTH = 4.05
SIZES = (("y", 4), ("xh", 2), ("core", 2), ("xl", 2), ("z1", 4), ("z0", 4))
BAND = ("y", "xh", "core")
PENCIL = ("xl", "z1", "z0")
NEAR = ("xl", "z0")
BF16 = jnp.bfloat16
F32 = jnp.float32
LANES = 128
ROWS = 8
REACH = 3
VMEM = pl.BlockSpec(memory_space=pltpu.VMEM)
SMEM = pl.BlockSpec(memory_space=pltpu.SMEM)
PARAMS = pltpu.CompilerParams(vmem_limit_bytes=16 * 2**20)


def halos(shard):
    size = lax.axis_size(PENCIL)
    up = [(i, (i + 1) % size) for i in range(size)]
    down = [(j, i) for i, j in up]
    return lax.ppermute(shard, PENCIL, up), lax.ppermute(shard, PENCIL, down)


def stencil_kernel(second, before, mid, after, pot, *rest):
    if second:
        start, out, ext = rest
    else:
        out, ext = rest
    width = mid.shape[1]
    slices = width // LANES
    ext[:, :width] = before[...].astype(F32)
    ext[:, width : 2 * width] = mid[...].astype(F32)
    ext[:, 2 * width :] = after[...].astype(F32)
    factor = 2.0 if second else 1.0
    centre = (pot[...] - 1.5 * WEIGHTS[0] - CENTRE) * (factor / HALFWIDTH)

    def at(index):
        return ext[:, index * LANES : (index + 1) * LANES]

    for s in range(slices):
        plane, row = divmod(s, ROWS)
        own = at(slices + s)
        total = centre[s : s + 1, :] * own
        for dist in range(1, REACH + 1):
            near = at(slices + s + ROWS * dist) + at(slices + s - ROWS * dist)
            base = slices + plane * ROWS
            near = near + at(base + (row + dist) % ROWS) + at(base + (row - dist) % ROWS)
            near = near + pltpu.roll(own, dist, 1) + pltpu.roll(own, LANES - dist, 1)
            total = total + (-0.5 * factor * WEIGHTS[dist] / HALFWIDTH) * near
        cells = slice(s * LANES, (s + 1) * LANES)
        if second:
            total = total - start[:, cells].astype(F32)
        out[:, cells] = total.astype(BF16)


def stencil(before, mid, after, pot, start=None):
    args = [before, mid, after, pot] + ([] if start is None else [start])
    return pl.pallas_call(
        functools.partial(stencil_kernel, start is not None),
        out_shape=jax.ShapeDtypeStruct(mid.shape, BF16),
        in_specs=[VMEM] * len(args),
        out_specs=VMEM,
        scratch_shapes=[pltpu.VMEM((mid.shape[0], 3 * mid.shape[1]), F32)],
        compiler_params=PARAMS,
        cost_estimate=pl.CostEstimate(flops=8_000_000, bytes_accessed=2_000_000, transcendentals=0),
        name="stencil_second" if start is not None else "stencil_first",
    )(*args)


def share_kernel(pieces, out):
    total = jnp.sum(pieces[...].astype(F32), axis=0).astype(BF16)
    for k in range(out.shape[0]):
        out[k] = total


def coef_kernel(scale, plan, place, pieces, out):
    total = jnp.sum(pieces[...].astype(F32), axis=0) * scale
    y, xh, core = place[0], place[1], place[2]
    turn = plan[4 * y + 2 * xh + core]
    bands = plan.shape[0]
    orbitals = total.shape[1] // bands
    low = lax.broadcasted_iota(jnp.int32, (total.shape[0], LANES), 1) < orbitals

    def earlier(block):
        group, source = divmod(block, bands // 4)
        side = xh if group < 2 else 1 - xh
        parity = core if group % 2 == 0 else 1 - core
        return (plan[4 * source + 2 * side + parity] < turn).astype(jnp.int32)

    for c in range(total.shape[1] // LANES):
        keep = jnp.where(low, earlier(2 * c), earlier(2 * c + 1)) > 0
        cells = slice(c * LANES, (c + 1) * LANES)
        part = jnp.where(keep, total[:, cells], 0.0).astype(BF16)
        for k in range(out.shape[0]):
            out[k, :, cells] = part


def widen(block):
    return jnp.broadcast_to(block[None], (lax.axis_size("y"),) + block.shape)


def along_y(wide):
    return lax.all_to_all(wide, "y", 0, 0).reshape(-1, wide.shape[-1])


def swap_cores(block):
    return lax.ppermute(block, "core", [(0, 1), (1, 0)])


def body(panels, potential, plan):
    orbitals = panels.shape[0]
    rows = panels.reshape(orbitals, -1)
    pot = potential.reshape(-1, LANES)
    scale = 1.0 / (rows.shape[1] * lax.axis_size(PENCIL))
    near, far = lax.axis_size(NEAR), lax.axis_size("z1")
    before, after = halos(rows)
    swapped = lax.ppermute(rows, "xh", [(0, 1), (1, 0)])
    same = along_y(widen(rows))
    wide = widen(swapped)
    before, after, wide = lax.optimization_barrier((before, after, wide))
    other = along_y(wide)
    first = stencil(before, rows, after, pot)
    before, after = halos(first)
    same_core = swap_cores(same)
    other, before, after = lax.optimization_barrier((other, before, after))
    other_core = swap_cores(other)
    filtered = stencil(before, first, after, pot, rows)
    blocks = [same, same_core, other, other_core]

    def margins(other):
        return lax.dot_general(
            filtered, other, (((1,), (1,)), ((), ())), preferred_element_type=F32
        ).astype(BF16)

    partial = jnp.concatenate([margins(block) for block in blocks], axis=1)
    pieces = lax.all_to_all(partial.reshape(near, orbitals // near, -1), NEAR, 0, 0)
    share = (orbitals // near, partial.shape[1])
    shares = pl.pallas_call(
        share_kernel,
        out_shape=jax.ShapeDtypeStruct((far,) + share, BF16),
        in_specs=[VMEM],
        out_specs=VMEM,
        compiler_params=PARAMS,
        name="share",
    )(pieces)
    shares = lax.all_to_all(shares, "z1", 0, 0)
    place = jnp.stack([lax.axis_index(a) for a in BAND]).astype(jnp.int32)
    coef = pl.pallas_call(
        functools.partial(coef_kernel, scale),
        out_shape=jax.ShapeDtypeStruct((near,) + share, BF16),
        in_specs=[SMEM, SMEM, VMEM],
        out_specs=VMEM,
        compiler_params=PARAMS,
        name="coef",
    )(plan, place, shares)
    coef = lax.all_to_all(coef, NEAR, 0, 0).reshape(orbitals, -1)
    width = same.shape[0]
    removed = jnp.zeros(rows.shape, F32)
    for k, block in enumerate(blocks):
        removed = removed + lax.dot_general(
            coef[:, k * width : (k + 1) * width], block, (((1,), (0,)), ((), ())),
            preferred_element_type=F32,
        )
    result = (filtered.astype(F32) - removed).astype(BF16)
    return result.reshape(panels.shape)


def solution(mesh):
    fine = Mesh(mesh.devices.reshape([s for _, s in SIZES]), [n for n, _ in SIZES])
    in_specs = (P(BAND, PENCIL, None, None), P(PENCIL, None, None), P())
    out_specs = P(BAND, PENCIL, None, None)
    return jax.shard_map(body, mesh=fine, in_specs=in_specs, out_specs=out_specs, check_vma=False)
```

```python
import functools

import jax
import jax.numpy as jnp
from jax import lax
from jax.experimental import pallas as pl
from jax.experimental.pallas import tpu as pltpu
from jax.sharding import Mesh, PartitionSpec as P

WEIGHTS = (-49.0 / 18.0, 1.5, -0.15, 1.0 / 90.0)
CENTRE = 6.05
HALFWIDTH = 4.05
SIZES = (("y", 4), ("xh", 2), ("core", 2), ("xl", 2), ("z1", 4), ("z0", 4))
BAND = ("y", "xh", "core")
PENCIL = ("xl", "z1", "z0")
NEAR = ("xl", "z0")
BF16 = jnp.bfloat16
F32 = jnp.float32
LANES = 128
ROWS = 8
REACH = 3
VMEM = pl.BlockSpec(memory_space=pltpu.VMEM)
SMEM = pl.BlockSpec(memory_space=pltpu.SMEM)
PARAMS = pltpu.CompilerParams(vmem_limit_bytes=16 * 2**20)


def halos(shard):
    size = lax.axis_size(PENCIL)
    up = [(i, (i + 1) % size) for i in range(size)]
    down = [(j, i) for i, j in up]
    return lax.ppermute(shard, PENCIL, up), lax.ppermute(shard, PENCIL, down)


def stencil_kernel(second, before, mid, after, pot, *rest):
    if second:
        start, out, ext = rest
    else:
        out, ext = rest
    width = mid.shape[1]
    slices = width // LANES
    ext[:, :width] = before[...].astype(F32)
    ext[:, width : 2 * width] = mid[...].astype(F32)
    ext[:, 2 * width :] = after[...].astype(F32)
    factor = 2.0 if second else 1.0
    centre = (pot[...] - 1.5 * WEIGHTS[0] - CENTRE) * (factor / HALFWIDTH)

    def at(index):
        return ext[:, index * LANES : (index + 1) * LANES]

    for s in range(slices):
        plane, row = divmod(s, ROWS)
        own = at(slices + s)
        total = centre[s : s + 1, :] * own
        for dist in range(1, REACH + 1):
            near = at(slices + s + ROWS * dist) + at(slices + s - ROWS * dist)
            base = slices + plane * ROWS
            near = near + at(base + (row + dist) % ROWS) + at(base + (row - dist) % ROWS)
            near = near + pltpu.roll(own, dist, 1) + pltpu.roll(own, LANES - dist, 1)
            total = total + (-0.5 * factor * WEIGHTS[dist] / HALFWIDTH) * near
        cells = slice(s * LANES, (s + 1) * LANES)
        if second:
            total = total - start[:, cells].astype(F32)
        out[:, cells] = total.astype(BF16)


def stencil(before, mid, after, pot, flops, start=None):
    args = [before, mid, after, pot] + ([] if start is None else [start])
    return pl.pallas_call(
        functools.partial(stencil_kernel, start is not None),
        out_shape=jax.ShapeDtypeStruct(mid.shape, BF16),
        in_specs=[VMEM] * len(args),
        out_specs=VMEM,
        scratch_shapes=[pltpu.VMEM((mid.shape[0], 3 * mid.shape[1]), F32)],
        compiler_params=PARAMS,
        cost_estimate=pl.CostEstimate(flops=flops, bytes_accessed=2_000_000, transcendentals=0),
        name="stencil_second" if start is not None else "stencil_first",
    )(*args)


def share_kernel(pieces, out):
    total = jnp.sum(pieces[...].astype(F32), axis=0).astype(BF16)
    for k in range(out.shape[0]):
        out[k] = total


def coef_kernel(scale, plan, place, pieces, out):
    total = jnp.sum(pieces[...].astype(F32), axis=0) * scale
    y, xh, core = place[0], place[1], place[2]
    turn = plan[4 * y + 2 * xh + core]
    bands = plan.shape[0]
    orbitals = total.shape[1] // bands
    low = lax.broadcasted_iota(jnp.int32, (total.shape[0], LANES), 1) < orbitals

    def earlier(block):
        group, source = divmod(block, bands // 4)
        side = xh if group < 2 else 1 - xh
        source = (y + (0, 3, 1, 2)[source]) % 4
        parity = core if group % 2 == 0 else 1 - core
        return (plan[4 * source + 2 * side + parity] < turn).astype(jnp.int32)

    for c in range(total.shape[1] // LANES):
        keep = jnp.where(low, earlier(2 * c), earlier(2 * c + 1)) > 0
        cells = slice(c * LANES, (c + 1) * LANES)
        part = jnp.where(keep, total[:, cells], 0.0).astype(BF16)
        for k in range(out.shape[0]):
            out[k, :, cells] = part


def widen(block):
    return jnp.broadcast_to(block[None], (lax.axis_size("y"),) + block.shape)


def stack_kernel(*refs):
    *blocks, out = refs
    rows = blocks[0].shape[0]
    for k, block in enumerate(blocks):
        out[k * rows : (k + 1) * rows, :] = block[...]


def stacked(blocks, flops):
    rows, cells = blocks[0].shape
    return pl.pallas_call(
        stack_kernel,
        out_shape=jax.ShapeDtypeStruct((len(blocks) * rows, cells), blocks[0].dtype),
        in_specs=[VMEM] * len(blocks),
        out_specs=VMEM,
        compiler_params=PARAMS,
        cost_estimate=pl.CostEstimate(flops=flops, bytes_accessed=2_000_000, transcendentals=0),
        name="stack",
    )(*blocks)


def along_y(wide):
    return lax.all_to_all(wide, "y", 0, 0).reshape(-1, wide.shape[-1])


def swap(axis, block):
    return lax.ppermute(block, axis, [(0, 1), (1, 0)])


def body(panels, potential, plan):
    orbitals = panels.shape[0]
    rows = panels.reshape(orbitals, -1)
    pot = potential.reshape(-1, LANES)
    scale = 1.0 / (rows.shape[1] * lax.axis_size(PENCIL))
    near, far = lax.axis_size(NEAR), lax.axis_size("z1")
    swapped = stacked([swap("xh", rows)], 100_000_000_000)
    same = stacked([rows] + [
        lax.ppermute(rows, "y", [(i, (i + step) % 4) for i in range(4)]) for step in (1, 3, 2)
    ], 8_000_000)
    before, after = halos(rows)
    first = stencil(before, rows, after, pot, 8000000)
    before, after = halos(first)
    low_y, high_y, opposite = (
        lax.ppermute(swapped, "y", [(i, (i + step) % 4) for i in range(4)]) for step in (1, 3, 2)
    )
    before, after, low_y, high_y, opposite = lax.optimization_barrier(
        (before, after, low_y, high_y, opposite)
    )
    filtered = stencil(before, first, after, pot, 8000000, rows)
    same_core = swap("core", same)
    other = jnp.concatenate([swapped, low_y, high_y, opposite], axis=0)
    other_core = swap("core", other)
    blocks = [same, same_core, other, other_core]

    def margins(other):
        return lax.dot_general(
            filtered, other, (((1,), (1,)), ((), ())), preferred_element_type=F32
        ).astype(BF16)

    partial = jnp.concatenate([margins(block) for block in blocks], axis=1)
    pieces = lax.all_to_all(partial.reshape(near, orbitals // near, -1), NEAR, 0, 0)
    share = (orbitals // near, partial.shape[1])
    shares = pl.pallas_call(
        share_kernel,
        out_shape=jax.ShapeDtypeStruct((far,) + share, BF16),
        in_specs=[VMEM],
        out_specs=VMEM,
        compiler_params=PARAMS,
        name="share",
    )(pieces)
    shares = lax.all_to_all(shares, "z1", 0, 0)
    place = jnp.stack([lax.axis_index(a) for a in BAND]).astype(jnp.int32)
    coef = pl.pallas_call(
        functools.partial(coef_kernel, scale),
        out_shape=jax.ShapeDtypeStruct((near,) + share, BF16),
        in_specs=[SMEM, SMEM, VMEM],
        out_specs=VMEM,
        compiler_params=PARAMS,
        name="coef",
    )(plan, place, shares)
    coef = lax.all_to_all(coef, NEAR, 0, 0).reshape(orbitals, -1)
    width = same.shape[0]
    removed = jnp.zeros(rows.shape, F32)
    for k, block in enumerate(blocks):
        removed = removed + lax.dot_general(
            coef[:, k * width : (k + 1) * width], block, (((1,), (0,)), ((), ())),
            preferred_element_type=F32,
        )
    result = (filtered.astype(F32) - removed).astype(BF16)
    return result.reshape(panels.shape)


def solution(mesh):
    fine = Mesh(mesh.devices.reshape([s for _, s in SIZES]), [n for n, _ in SIZES])
    in_specs = (P(BAND, PENCIL, None, None), P(PENCIL, None, None), P())
    out_specs = P(BAND, PENCIL, None, None)
    return jax.shard_map(body, mesh=fine, in_specs=in_specs, out_specs=out_specs, check_vma=False)
```

```python
import functools

import jax
import jax.numpy as jnp
from jax import lax
from jax.experimental import pallas as pl
from jax.experimental.pallas import tpu as pltpu
from jax.sharding import Mesh, PartitionSpec as P

WEIGHTS = (-49.0 / 18.0, 1.5, -0.15, 1.0 / 90.0)
CENTRE = 6.05
HALFWIDTH = 4.05
SIZES = (("y", 4), ("xh", 2), ("core", 2), ("xl", 2), ("z1", 4), ("z0", 4))
BAND = ("y", "xh", "core")
PENCIL = ("xl", "z1", "z0")
NEAR = ("xl", "z0")
BF16 = jnp.bfloat16
F32 = jnp.float32
LANES = 128
ROWS = 8
REACH = 3
VMEM = pl.BlockSpec(memory_space=pltpu.VMEM)
SMEM = pl.BlockSpec(memory_space=pltpu.SMEM)
PARAMS = pltpu.CompilerParams(vmem_limit_bytes=16 * 2**20)


def halos(shard):
    size = lax.axis_size(PENCIL)
    up = [(i, (i + 1) % size) for i in range(size)]
    down = [(j, i) for i, j in up]
    return lax.ppermute(shard, PENCIL, up), lax.ppermute(shard, PENCIL, down)


def stencil_kernel(second, before, mid, after, pot, *rest):
    if second:
        start, out, ext = rest
    else:
        out, ext = rest
    width = mid.shape[1]
    slices = width // LANES
    ext[:, :width] = before[...].astype(F32)
    ext[:, width : 2 * width] = mid[...].astype(F32)
    ext[:, 2 * width :] = after[...].astype(F32)
    factor = 2.0 if second else 1.0
    centre = (pot[...] - 1.5 * WEIGHTS[0] - CENTRE) * (factor / HALFWIDTH)

    def at(index):
        return ext[:, index * LANES : (index + 1) * LANES]

    for s in range(slices):
        plane, row = divmod(s, ROWS)
        own = at(slices + s)
        total = centre[s : s + 1, :] * own
        for dist in range(1, REACH + 1):
            near = at(slices + s + ROWS * dist) + at(slices + s - ROWS * dist)
            base = slices + plane * ROWS
            near = near + at(base + (row + dist) % ROWS) + at(base + (row - dist) % ROWS)
            near = near + pltpu.roll(own, dist, 1) + pltpu.roll(own, LANES - dist, 1)
            total = total + (-0.5 * factor * WEIGHTS[dist] / HALFWIDTH) * near
        cells = slice(s * LANES, (s + 1) * LANES)
        if second:
            total = total - start[:, cells].astype(F32)
        out[:, cells] = total.astype(BF16)


def stencil(before, mid, after, pot, flops, start=None):
    args = [before, mid, after, pot] + ([] if start is None else [start])
    return pl.pallas_call(
        functools.partial(stencil_kernel, start is not None),
        out_shape=jax.ShapeDtypeStruct(mid.shape, BF16),
        in_specs=[VMEM] * len(args),
        out_specs=VMEM,
        scratch_shapes=[pltpu.VMEM((mid.shape[0], 3 * mid.shape[1]), F32)],
        compiler_params=PARAMS,
        cost_estimate=pl.CostEstimate(flops=flops, bytes_accessed=2_000_000, transcendentals=0),
        name="stencil_second" if start is not None else "stencil_first",
    )(*args)


def share_kernel(pieces, out):
    total = jnp.sum(pieces[...].astype(F32), axis=0).astype(BF16)
    for k in range(out.shape[0]):
        out[k] = total


def coef_kernel(scale, plan, place, pieces, out):
    total = jnp.sum(pieces[...].astype(F32), axis=0) * scale
    y, xh, core = place[0], place[1], place[2]
    turn = plan[4 * y + 2 * xh + core]
    bands = plan.shape[0]
    orbitals = total.shape[1] // bands
    low = lax.broadcasted_iota(jnp.int32, (total.shape[0], LANES), 1) < orbitals

    def earlier(block):
        group, source = divmod(block, bands // 4)
        side = xh if group < 2 else 1 - xh
        source = (y + (0, 3, 1, 2)[source]) % 4
        parity = core if group % 2 == 0 else 1 - core
        return (plan[4 * source + 2 * side + parity] < turn).astype(jnp.int32)

    for c in range(total.shape[1] // LANES):
        keep = jnp.where(low, earlier(2 * c), earlier(2 * c + 1)) > 0
        cells = slice(c * LANES, (c + 1) * LANES)
        part = jnp.where(keep, total[:, cells], 0.0).astype(BF16)
        for k in range(out.shape[0]):
            out[k, :, cells] = part


def widen(block):
    return jnp.broadcast_to(block[None], (lax.axis_size("y"),) + block.shape)


def stack_kernel(*refs):
    *blocks, out = refs
    rows = blocks[0].shape[0]
    for k, block in enumerate(blocks):
        out[k * rows : (k + 1) * rows, :] = block[...]


def stacked(blocks, flops):
    rows, cells = blocks[0].shape
    return pl.pallas_call(
        stack_kernel,
        out_shape=jax.ShapeDtypeStruct((len(blocks) * rows, cells), blocks[0].dtype),
        in_specs=[VMEM] * len(blocks),
        out_specs=VMEM,
        compiler_params=PARAMS,
        cost_estimate=pl.CostEstimate(flops=flops, bytes_accessed=2_000_000, transcendentals=0),
        name="stack",
    )(*blocks)


def along_y(wide):
    return lax.all_to_all(wide, "y", 0, 0).reshape(-1, wide.shape[-1])


def swap(axis, block):
    return lax.ppermute(block, axis, [(0, 1), (1, 0)])


def body(panels, potential, plan):
    orbitals = panels.shape[0]
    rows = panels.reshape(orbitals, -1)
    pot = potential.reshape(-1, LANES)
    scale = 1.0 / (rows.shape[1] * lax.axis_size(PENCIL))
    near, far = lax.axis_size(NEAR), lax.axis_size("z1")
    swapped = stacked([swap("xh", rows)], 100_000_000_000)
    same = stacked([rows] + [
        lax.ppermute(rows, "y", [(i, (i + step) % 4) for i in range(4)]) for step in (1, 3, 2)
    ], 8_000_000)
    before, after = halos(rows)
    first = stencil(before, rows, after, pot, 8000000)
    before, after = halos(first)
    low_y, high_y, opposite = (
        lax.ppermute(swapped, "y", [(i, (i + step) % 4) for i in range(4)]) for step in (1, 3, 2)
    )
    before, after, low_y, high_y, opposite = lax.optimization_barrier(
        (before, after, low_y, high_y, opposite)
    )
    filtered = stencil(before, first, after, pot, 8000000, rows)
    same_core = swap("core", same)
    other = jnp.concatenate([swapped, low_y, high_y, opposite], axis=0)
    other_core = swap("core", other)
    blocks = [same, same_core, other, other_core]

    def margins(other):
        return lax.dot_general(
            filtered, other, (((1,), (1,)), ((), ())), preferred_element_type=F32
        ).astype(BF16)

    partial = jnp.concatenate([margins(block) for block in blocks], axis=1)
    pieces = lax.all_to_all(partial.reshape(near, orbitals // near, -1), NEAR, 0, 0)
    share = (orbitals // near, partial.shape[1])
    shares = pl.pallas_call(
        share_kernel,
        out_shape=jax.ShapeDtypeStruct((far,) + share, BF16),
        in_specs=[VMEM],
        out_specs=VMEM,
        compiler_params=PARAMS,
        name="share",
    )(pieces)
    shares = lax.all_to_all(shares, "z1", 0, 0)
    place = jnp.stack([lax.axis_index(a) for a in BAND]).astype(jnp.int32)
    coef = pl.pallas_call(
        functools.partial(coef_kernel, scale),
        out_shape=jax.ShapeDtypeStruct((near,) + share, BF16),
        in_specs=[SMEM, SMEM, VMEM],
        out_specs=VMEM,
        compiler_params=PARAMS,
        name="coef",
    )(plan, place, shares)
    coef = lax.all_to_all(coef, NEAR, 0, 0).reshape(orbitals, -1)
    width = same.shape[0]
    removed = jnp.zeros(rows.shape, F32)
    for k, block in reversed(list(enumerate(blocks))):
        removed = removed + lax.dot_general(
            coef[:, k * width : (k + 1) * width], block, (((1,), (0,)), ((), ())),
            preferred_element_type=F32,
        )
    result = (filtered.astype(F32) - removed).astype(BF16)
    return result.reshape(panels.shape)


def solution(mesh):
    fine = Mesh(mesh.devices.reshape([s for _, s in SIZES]), [n for n, _ in SIZES])
    in_specs = (P(BAND, PENCIL, None, None), P(PENCIL, None, None), P())
    out_specs = P(BAND, PENCIL, None, None)
    return jax.shard_map(body, mesh=fine, in_specs=in_specs, out_specs=out_specs, check_vma=False)
```

```python
import functools

import jax
import jax.numpy as jnp
from jax import lax
from jax.experimental import pallas as pl
from jax.experimental.pallas import tpu as pltpu
from jax.sharding import Mesh, PartitionSpec as P

WEIGHTS = (-49.0 / 18.0, 1.5, -0.15, 1.0 / 90.0)
CENTRE = 6.05
HALFWIDTH = 4.05
SIZES = (("y", 4), ("xh", 2), ("core", 2), ("xl", 2), ("z1", 4), ("z0", 4))
BAND = ("y", "xh", "core")
PENCIL = ("xl", "z1", "z0")
NEAR = ("xl", "z0")
BF16 = jnp.bfloat16
F32 = jnp.float32
LANES = 128
ROWS = 8
REACH = 3
VMEM = pl.BlockSpec(memory_space=pltpu.VMEM)
SMEM = pl.BlockSpec(memory_space=pltpu.SMEM)
PARAMS = pltpu.CompilerParams(vmem_limit_bytes=16 * 2**20)


def halos(shard):
    size = lax.axis_size(PENCIL)
    up = [(i, (i + 1) % size) for i in range(size)]
    down = [(j, i) for i, j in up]
    return lax.ppermute(shard, PENCIL, up), lax.ppermute(shard, PENCIL, down)


def stencil_kernel(second, before, mid, after, pot, *rest):
    if second:
        start, out, ext = rest
    else:
        out, ext = rest
    width = mid.shape[1]
    slices = width // LANES
    ext[:, :width] = before[...].astype(F32)
    ext[:, width : 2 * width] = mid[...].astype(F32)
    ext[:, 2 * width :] = after[...].astype(F32)
    factor = 2.0 if second else 1.0
    centre = (pot[...] - 1.5 * WEIGHTS[0] - CENTRE) * (factor / HALFWIDTH)

    def at(index):
        return ext[:, index * LANES : (index + 1) * LANES]

    for s in range(slices):
        plane, row = divmod(s, ROWS)
        own = at(slices + s)
        total = centre[s : s + 1, :] * own
        for dist in range(1, REACH + 1):
            near = at(slices + s + ROWS * dist) + at(slices + s - ROWS * dist)
            base = slices + plane * ROWS
            near = near + at(base + (row + dist) % ROWS) + at(base + (row - dist) % ROWS)
            near = near + pltpu.roll(own, dist, 1) + pltpu.roll(own, LANES - dist, 1)
            total = total + (-0.5 * factor * WEIGHTS[dist] / HALFWIDTH) * near
        cells = slice(s * LANES, (s + 1) * LANES)
        if second:
            total = total - start[:, cells].astype(F32)
        out[:, cells] = total.astype(BF16)


def stencil(before, mid, after, pot, flops, start=None):
    args = [before, mid, after, pot] + ([] if start is None else [start])
    return pl.pallas_call(
        functools.partial(stencil_kernel, start is not None),
        out_shape=jax.ShapeDtypeStruct(mid.shape, BF16),
        in_specs=[VMEM] * len(args),
        out_specs=VMEM,
        scratch_shapes=[pltpu.VMEM((mid.shape[0], 3 * mid.shape[1]), F32)],
        compiler_params=PARAMS,
        cost_estimate=pl.CostEstimate(flops=flops, bytes_accessed=2_000_000, transcendentals=0),
        name="stencil_second" if start is not None else "stencil_first",
    )(*args)


def share_kernel(pieces, out):
    total = jnp.sum(pieces[...].astype(F32), axis=0).astype(BF16)
    for k in range(out.shape[0]):
        out[k] = total


def coef_kernel(scale, plan, place, pieces, out):
    total = jnp.sum(pieces[...].astype(F32), axis=0) * scale
    y, xh, core = place[0], place[1], place[2]
    turn = plan[4 * y + 2 * xh + core]
    bands = plan.shape[0]
    orbitals = total.shape[1] // bands
    low = lax.broadcasted_iota(jnp.int32, (total.shape[0], LANES), 1) < orbitals

    def earlier(block):
        group, source = divmod(block, bands // 4)
        side = xh if group < 2 else 1 - xh
        source = (y + (0, 3, 1, 2)[source]) % 4
        parity = core if group % 2 == 0 else 1 - core
        return (plan[4 * source + 2 * side + parity] < turn).astype(jnp.int32)

    for c in range(total.shape[1] // LANES):
        keep = jnp.where(low, earlier(2 * c), earlier(2 * c + 1)) > 0
        cells = slice(c * LANES, (c + 1) * LANES)
        part = jnp.where(keep, total[:, cells], 0.0).astype(BF16)
        for k in range(out.shape[0]):
            out[k, :, cells] = part


def widen(block):
    return jnp.broadcast_to(block[None], (lax.axis_size("y"),) + block.shape)


def stack_kernel(*refs):
    *blocks, out = refs
    rows = blocks[0].shape[0]
    for k, block in enumerate(blocks):
        out[k * rows : (k + 1) * rows, :] = block[...]


def stacked(blocks, flops):
    rows, cells = blocks[0].shape
    return pl.pallas_call(
        stack_kernel,
        out_shape=jax.ShapeDtypeStruct((len(blocks) * rows, cells), blocks[0].dtype),
        in_specs=[VMEM] * len(blocks),
        out_specs=VMEM,
        compiler_params=PARAMS,
        cost_estimate=pl.CostEstimate(flops=flops, bytes_accessed=2_000_000, transcendentals=0),
        name="stack",
    )(*blocks)


def along_y(wide):
    return lax.all_to_all(wide, "y", 0, 0).reshape(-1, wide.shape[-1])


def swap(axis, block):
    return lax.ppermute(block, axis, [(0, 1), (1, 0)])


def body(panels, potential, plan):
    orbitals = panels.shape[0]
    rows = panels.reshape(orbitals, -1)
    pot = potential.reshape(-1, LANES)
    scale = 1.0 / (rows.shape[1] * lax.axis_size(PENCIL))
    near, far = lax.axis_size(NEAR), lax.axis_size("z1")
    swapped = stacked([swap("xh", rows)], 100_000_000_000)
    same = stacked([rows] + [
        lax.ppermute(rows, "y", [(i, (i + step) % 4) for i in range(4)]) for step in (1, 3, 2)
    ], 8_000_000)
    before, after = halos(rows)
    first = stencil(before, rows, after, pot, 8000000)
    before, after = halos(first)
    low_y, high_y, opposite = (
        lax.ppermute(swapped, "y", [(i, (i + step) % 4) for i in range(4)]) for step in (1, 3, 2)
    )
    place = jnp.stack([lax.axis_index(a) for a in BAND]).astype(jnp.int32)
    before, after, low_y, high_y, opposite, place = lax.optimization_barrier(
        (before, after, low_y, high_y, opposite, place)
    )
    filtered = stencil(before, first, after, pot, 8000000, rows)
    same_core = swap("core", same)
    other = jnp.concatenate([swapped, low_y, high_y, opposite], axis=0)
    other_core = swap("core", other)
    blocks = [same, same_core, other, other_core]

    def margins(other):
        return lax.dot_general(
            filtered, other, (((1,), (1,)), ((), ())), preferred_element_type=F32
        ).astype(BF16)

    partial = jnp.concatenate([margins(block) for block in blocks], axis=1)
    pieces = lax.all_to_all(partial.reshape(near, orbitals // near, -1), NEAR, 0, 0)
    share = (orbitals // near, partial.shape[1])
    shares = pl.pallas_call(
        share_kernel,
        out_shape=jax.ShapeDtypeStruct((far,) + share, BF16),
        in_specs=[VMEM],
        out_specs=VMEM,
        compiler_params=PARAMS,
        name="share",
    )(pieces)
    shares = lax.all_to_all(shares, "z1", 0, 0)
    coef = pl.pallas_call(
        functools.partial(coef_kernel, scale),
        out_shape=jax.ShapeDtypeStruct((near,) + share, BF16),
        in_specs=[SMEM, SMEM, VMEM],
        out_specs=VMEM,
        compiler_params=PARAMS,
        name="coef",
    )(plan, place, shares)
    coef = lax.all_to_all(coef, NEAR, 0, 0).reshape(orbitals, -1)
    width = same.shape[0]
    removed = jnp.zeros(rows.shape, F32)
    for k, block in reversed(list(enumerate(blocks))):
        removed = removed + lax.dot_general(
            coef[:, k * width : (k + 1) * width], block, (((1,), (0,)), ((), ())),
            preferred_element_type=F32,
        )
    result = (filtered.astype(F32) - removed).astype(BF16)
    return result.reshape(panels.shape)


def solution(mesh):
    fine = Mesh(mesh.devices.reshape([s for _, s in SIZES]), [n for n, _ in SIZES])
    in_specs = (P(BAND, PENCIL, None, None), P(PENCIL, None, None), P())
    out_specs = P(BAND, PENCIL, None, None)
    return jax.shard_map(body, mesh=fine, in_specs=in_specs, out_specs=out_specs, check_vma=False)
```
